128 devices in a mesh: grid: 32 (over x_lo, z, y), mem: 4 (over x_hi, core).
Axes of the slice: x: 4 (x_hi: 2, x_lo: 2; x = x_hi * 2 + x_lo), y: 4, z: 4, core: 2. Of those that a mesh axis runs over, the one named last changes fastest.
Arguments:
- field: bfloat16 [512, 2, 512, 1024], P('mem', None, 'grid'), may hold values from -6 to 6
- winds: bfloat16 [2, 2, 512, 1024], P(None, None, 'grid'), may hold values from -0.44921875 to 0.44921875
- obs_index: int32 [512, 3072], P('grid'), may hold values from 0 to 524287, as said below
- measured_values: float32 [512, 3072], P('grid'), may hold values from -6 to 6
- precision_weights: float32 [512, 3072], P('grid'), may hold values from 0.05 to 1
Outputs:
- gram: float32 [512, 512, 512], P('grid', 'mem')
- proj: float32 [512, 512], P('grid', 'mem')
The draws below stay inside these ranges and needn't reach their ends.
Inputs may be any that keep to these rules, and one draw needn't show every extreme that they name: obs_index holds row * 1024 + column; an observation of patch p lies in rows (p // 16) * 16 - 8 to (p // 16 + 1) * 16 + 7 and columns (p % 16) * 64 - 8 to (p % 16 + 1) * 64 + 7, clipped to the grid; cells may repeat.
All inputs are finite; a program needn't handle non-finite values.
Results may differ from the reference program's by a relative error of at most 0.005.
Values may be sent and summed in bfloat16 or wider, within the bound.
No kernel may reach another device: no remote copies, remote signals or barrier semaphores. Data moves between devices by JAX's collectives and lax.ppermute only.
A program may use at most 320 MiB of HBM per device.

```python
import math
import jax
import jax.numpy as jnp
from jax import lax

MEMBERS = 512
CX = 16
NY = 1024
PATCH_C = 64
HALO_R = 8
K = 3072
NX = 512
NPC = 16
PATCHES = 512


def draw_obs_index(key, part):
    key = jax.random.fold_in(key, 11)
    patch = jnp.arange(PATCHES, dtype=jnp.int32)
    strip = patch // NPC
    column_block = patch % NPC
    row_low = jnp.maximum(strip * CX - HALO_R, 0)
    row_high = jnp.minimum((strip + 1) * CX + HALO_R, NX)
    col_low = jnp.maximum(column_block * PATCH_C - HALO_R, 0)
    col_high = jnp.minimum((column_block + 1) * PATCH_C + HALO_R, NY)
    key_rows, key_cols = jax.random.split(key)
    rows_drawn = jax.random.randint(key_rows, (PATCHES, K), row_low[:, None], row_high[:, None], dtype=jnp.int32)
    cols_drawn = jax.random.randint(key_cols, (PATCHES, K), col_low[:, None], col_high[:, None], dtype=jnp.int32)
    cells = (rows_drawn * NY + cols_drawn).astype(jnp.int32)
    cells = cells.at[0, 0].set(jnp.int32(0))
    cells = cells.at[PATCHES - 1, K - 1].set(jnp.int32(NX * NY - 1))
    return cells


def level_of(stream_key, extent, shards, least, top_value):
    def one(axis_at, shards_of):
        heights = jax.random.uniform(jax.random.fold_in(jax.random.fold_in(stream_key, 6), axis_at), (shards_of,), jnp.float32, least / len(shards), top_value / len(shards))
        return jnp.repeat(jnp.exp(heights), extent[axis_at] // shards_of).reshape((-1,) + (1,) * (len(extent) - axis_at - 1))

    level = one(*shards[0])
    for cut in shards[1:]:
        level = level * one(*cut)
    return level


def centred(stream_key, shape, deviation, reach, shards=(), kind=jnp.bfloat16):
    array = deviation * jax.random.normal(stream_key, shape, jnp.float32)
    if shards:
        array = array * level_of(stream_key, shape, shards, -0.22, 0.18)
    return jnp.clip(array, -reach, reach).astype(kind)


def setup_inputs(seed: int = 0) -> dict:
    arg_keys = jax.random.split(jax.random.key(seed), 6)
    return {
        "field": centred(arg_keys[0], (MEMBERS, 2, NX, NY), 1.0, 6.0, ((0, 4), (2, 32))),
        "winds": jnp.clip(jax.random.uniform(arg_keys[1], (2, 2, NX, NY), jnp.float32, -0.44921875, 0.44921875) * level_of(arg_keys[1], (2, 2, NX, NY), ((2, 32),), -0.4, 0.0), -0.44921875, 0.44921875).astype(jnp.bfloat16),
        "obs_index": draw_obs_index(jax.random.fold_in(arg_keys[5], 71), 0),
        "measured_values": centred(arg_keys[3], (PATCHES, K), 1.0, 6.0, ((0, 32),), jnp.float32),
        "precision_weights": jnp.clip(jnp.exp(math.log(1.0) - 2.9957323 * jax.random.uniform(arg_keys[4], (PATCHES, K), jnp.float32) ** level_of(arg_keys[4], (PATCHES, K), ((0, 32),), -0.2, 0.2)), 0.05, 1.0),
    }


LOC_AREA = 512.0
LOW_SHARE = 0.7
HIGH_SHARE = 0.3

def advect(state, flow_rows, flow_cols):
    widths = [(0, 0)] * (state.ndim - 2) + [(1, 1), (1, 1)]
    padded = jnp.pad(state, widths)
    above = padded[..., :-2, 1:-1]
    below = padded[..., 2:, 1:-1]
    left = padded[..., 1:-1, :-2]
    right = padded[..., 1:-1, 2:]
    return state - jnp.maximum(flow_rows, 0.0) * (state - above) - jnp.minimum(flow_rows, 0.0) * (below - state) - jnp.maximum(flow_cols, 0.0) * (state - left) - jnp.minimum(flow_cols, 0.0) * (right - state)

def reference(field, winds, obs_index, measured_values, precision_weights):
    flows = winds.astype(jnp.float32)

    def predicted_member(member_state):
        state = member_state.astype(jnp.float32)
        for step in range(2):
            state = advect(state, flows[0], flows[1])
        return (LOW_SHARE * state[0] + HIGH_SHARE * state[1]).astype(jnp.bfloat16)
    measured_field = lax.map(predicted_member, field)
    flat = measured_field.reshape(MEMBERS, NX * NY)
    patch = jnp.arange(PATCHES, dtype=jnp.int32)
    strip = patch // NPC
    column_block = patch % NPC
    centre_row = (strip * CX).astype(jnp.float32)[:, None] + (CX - 1) * 0.5
    centre_col = (column_block * PATCH_C).astype(jnp.float32)[:, None] + (PATCH_C - 1) * 0.5
    row_diff = (obs_index // NY).astype(jnp.float32) - centre_row
    col_diff = (obs_index % NY).astype(jnp.float32) - centre_col
    distance = row_diff * row_diff + col_diff * col_diff
    weight = precision_weights * jnp.exp(-distance / LOC_AREA)
    root = jnp.sqrt(weight / (MEMBERS - 1.0))

    def one_patch(items):
        index, root_patch, values = items
        seen = jnp.take(flat, index, axis=1)
        mean = lax.optimization_barrier(jnp.sum(seen.astype(jnp.float32), axis=0)) / MEMBERS
        scaled = (root_patch * (seen.astype(jnp.float32) - mean)).astype(jnp.bfloat16)
        innov = (root_patch * (values - mean)).astype(jnp.bfloat16)
        gram_patch = jnp.dot(scaled, scaled.T, preferred_element_type=jnp.float32)
        proj_patch = jnp.dot(scaled, innov, preferred_element_type=jnp.float32)
        return (gram_patch, proj_patch)
    gram, proj = lax.map(one_patch, (obs_index, root, measured_values))
    return (gram, proj)
```

```python
import functools

import jax
import jax.numpy as jnp
from jax import lax
from jax.experimental import pallas as pl
from jax.experimental.pallas import tpu as pltpu
from jax.sharding import PartitionSpec as P

PATCH_C = 64
HALO_R = 8
LOC_AREA = 512.0
LOW_SHARE = 0.7
HIGH_SHARE = 0.3

ROWS = 16
WIDTH = 1024
MINE = 128
GROUPS = 4
MEMBERS = MINE * GROUPS
LANES = 128
BLOCKS = WIDTH // LANES
TILE_M = 64
INNER = 13
OUTER = 5
OWN_PATCHES = 4
K = 3072
PAIR = 2
VMEM = 60 * 1024 * 1024
BF = jnp.bfloat16
F32 = jnp.float32


def lane_iota(rows):
    return lax.broadcasted_iota(jnp.int32, (rows, LANES), 1)


def row_choice(picked, row_of):
    shape = (picked * 16, 16 * ROWS)
    out = lax.broadcasted_iota(jnp.int32, shape, 0)
    source = (out & 15) * ROWS + row_of(lax.shift_right_logical(out, 4))
    return jnp.where(source == lax.broadcasted_iota(jnp.int32, shape, 1), 1.0, 0.0).astype(BF)


def choose_rows(choice, field, start, level):
    members = field[pl.ds(start, 16), level].reshape(16 * ROWS, WIDTH)
    return jnp.dot(choice, members, preferred_element_type=F32)


def edges_kernel(wind, field, top, bottom):
    step = pl.program_id(0)
    choice = row_choice(4, lambda r: jnp.where(r < 2, r, r + ROWS - 4))

    @pl.when(step == 0)
    def _():
        for pack, row in ((top, 0), (bottom, ROWS - 1)):
            winds = [
                wind[part, level].astype(F32)[row : row + 1] for part in range(2) for level in range(2)
            ]
            rows = jnp.concatenate(winds + [jnp.zeros((12, WIDTH), F32)], axis=0)
            pack[4 * MINE : 4 * MINE + 16] = rows.astype(BF)

    for group in range(TILE_M // 16):
        for level in range(2):
            rows = choose_rows(choice, field, group * 16, level).astype(BF)
            for i in range(2):
                at = pl.multiple_of((level * 2 + i) * MINE + step * TILE_M + group * 16, 16)
                top[pl.ds(at, 16)] = rows[i * 16 : (i + 1) * 16]
                bottom[pl.ds(at, 16)] = rows[32 + i * 16 : 48 + i * 16]


def edges(winds, field):
    pack = jax.ShapeDtypeStruct((4 * MINE + 16, WIDTH), BF)
    return pl.pallas_call(
        edges_kernel,
        grid=(MINE // TILE_M,),
        in_specs=[
            pl.BlockSpec((2, 2, ROWS, WIDTH), lambda i: (0, 0, 0, 0)),
            pl.BlockSpec((TILE_M, 2, ROWS, WIDTH), lambda i: (i, 0, 0, 0)),
        ],
        out_specs=[pl.BlockSpec(pack.shape, lambda i: (0, 0))] * 2,
        out_shape=[pack] * 2,
        compiler_params=pltpu.CompilerParams(vmem_limit_bytes=VMEM),
        cost_estimate=pl.CostEstimate(flops=10**7, bytes_accessed=10 * 2**20, transcendentals=0),
        name="edges",
    )(winds, field)


def observe_kernel(inner, sc, wind, field, *refs):
    if inner:
        rows = ROWS
    else:
        lows, low_wind = refs[0:4], refs[4]
        highs, high_wind = refs[5:9], refs[9]
        refs = refs[10:]
        rows = 12
    outs = refs[0:4]
    raw, once, coef, row_out, edge = refs[4:]
    me = sc[0]
    lane = lane_iota(TILE_M)
    first = lane_iota(8) == 0
    last = lane_iota(8) == LANES - 1

    @pl.when(pl.program_id(0) == 0)
    def _():
        column = lax.broadcasted_iota(jnp.int32, (1, WIDTH), 1)

        def coefs(a, b):
            up, down = jnp.maximum(a, 0.0), -jnp.minimum(a, 0.0)
            left, right = jnp.maximum(b, 0.0), -jnp.minimum(b, 0.0)
            centre = 1.0 - up - down - left - right
            left = jnp.where(column == 0, 0.0, left)
            right = jnp.where(column == WIDTH - 1, 0.0, right)
            return centre, up, down, left, right

        def put(at_row, level, arrays, r):
            for k, array in enumerate(arrays):
                coef[at_row, level * 5 + k] = jnp.broadcast_to(array[r : r + 1], (8, WIDTH))

        if inner:
            places = [(r, r) for r in range(1, ROWS - 1)]
        else:
            places = [(2, 0), (3, 1), (4, 2), (7, 13), (8, 14), (9, 15)]
        for level in range(2):
            arrays = coefs(wind[0, level].astype(F32), wind[1, level].astype(F32))
            for at_row, r in places:
                put(at_row, level, arrays, r)
            if not inner:
                for side, at_row in ((low_wind, 1), (high_wind, 10)):
                    winds = side[...].astype(F32)
                    put(at_row, level, coefs(winds[level : level + 1], winds[2 + level : 3 + level]), 0)
        row_out[0] = jnp.zeros((TILE_M, LANES), F32)
        row_out[BLOCKS + 1] = jnp.zeros((TILE_M, LANES), F32)

    if inner:
        picked, at_first, choice = ROWS, 0, row_choice(ROWS, lambda r: r)
    else:
        picked, at_first, choice = 8, 2, row_choice(8, lambda r: jnp.where(r < 4, r, r + 8))
        for level in range(2):
            for i in range(2):
                raw[level, i] = lows[level * 2 + i][...].astype(F32)
                raw[level, 10 + i] = highs[level * 2 + i][...].astype(F32)

    def reorder(group, carry):
        start = pl.multiple_of(group * 16, 16)
        for level in range(2):
            chosen = choose_rows(choice, field, start, level)
            for r in range(picked):
                raw[level, at_first + r, pl.ds(start, 16), :] = chosen[r * 16 : (r + 1) * 16]
        return carry

    lax.fori_loop(0, TILE_M // 16, reorder, 0)

    def stencil(src, level, row):
        tiles = range(TILE_M // 8)

        def block(at_row, m, j):
            return src[level, at_row, m * 8 : (m + 1) * 8, j * LANES : (j + 1) * LANES]

        here = [block(row, m, 0) for m in tiles]
        before = [None for m in tiles]
        turned_back = [pltpu.roll(here[m], LANES - 1, 1) for m in tiles]
        for j in range(BLOCKS):
            lanes = slice(j * LANES, (j + 1) * LANES)
            centre, up, down, west, east = (coef[row, level * 5 + k, :, lanes] for k in range(5))
            for m in tiles:
                turned = pltpu.roll(here[m], 1, 1)
                left = turned if j == 0 else jnp.where(first, before[m], turned)
                right = turned_back[m]
                after, after_back = None, None
                if j + 1 < BLOCKS:
                    after = block(row, m, j + 1)
                    after_back = pltpu.roll(after, LANES - 1, 1)
                    right = jnp.where(last, after_back, right)
                value = (
                    centre * here[m]
                    + up * block(row - 1, m, j)
                    + down * block(row + 1, m, j)
                    + west * left
                    + east * right
                )
                yield j, slice(m * 8, (m + 1) * 8), value
                before[m], here[m], turned_back[m] = turned, after, after_back

    def step_one(row, carry):
        for level in range(2):
            for j, members, value in stencil(raw, level, row):
                once[level, row, members, j * LANES : (j + 1) * LANES] = value
        return carry

    def step_two(row, base, slot):
        for j, members, value in stencil(once, 0, row):
            row_out[1 + j, members] = LOW_SHARE * value
        for j, members, value in stencil(once, 1, row):
            row_out[1 + j, members] = row_out[1 + j, members] + HIGH_SHARE * value
        for s in range(GROUPS):
            d = me ^ s
            for j in range(2):
                outs[s][base + j] = row_out[1 + 2 * d + j].astype(BF)
            outer = jnp.where(
                lane < HALO_R,
                row_out[2 * d + 3],
                jnp.where(lane >= LANES - HALO_R, row_out[2 * d], 0.0),
            )
            edge[s] = edge[s] + pltpu.roll(outer, HALO_R + 2 * HALO_R * slot, 1)

    def clear():
        for s in range(GROUPS):
            edge[s] = jnp.zeros((TILE_M, LANES), F32)

    def flush(at):
        for s in range(GROUPS):
            outs[s][at] = edge[s].astype(BF)

    if inner:
        lax.fori_loop(1, ROWS - 1, step_one, 0)
        for half in range(2):
            clear()

            def step(t, carry, half=half):
                step_two(2 + half * 6 + t, half * INNER + 2 * t, t)
                return carry

            lax.fori_loop(0, 6, step, 0)
            flush(half * INNER + 12)
    else:
        lax.fori_loop(1, 5, step_one, 0)
        lax.fori_loop(7, 11, step_one, 0)
        clear()

        def step(t, carry):
            under = t // 2
            step_two(2 + t + 4 * under, 2 * t + under, t)
            return carry

        lax.fori_loop(0, 4, step, 0)
        flush(4)


def observe(inner, scalars, winds, *arrays):
    steps = MINE // TILE_M
    wind_spec = pl.BlockSpec((2, 2, ROWS, WIDTH), lambda i, sc: (0, 0, 0, 0))
    specs = [pl.BlockSpec((TILE_M, 2, ROWS, WIDTH), lambda i, sc: (i, 0, 0, 0))]
    if inner:
        rows, blocks, work = ROWS, 2 * INNER, 7
        operands = arrays
    else:
        rows, blocks, work = 12, 9, 3
        side = [
            pl.BlockSpec((TILE_M, WIDTH), functools.partial(lambda k, i, sc: (k * steps + i, 0), k))
            for k in range(4)
        ] + [pl.BlockSpec((16, WIDTH), lambda i, sc: (4 * MINE // 16, 0))]
        specs = specs + side * 2
        field, low, high = arrays
        operands = [field] + [low] * 5 + [high] * 5
    return pl.pallas_call(
        functools.partial(observe_kernel, inner),
        grid_spec=pltpu.PrefetchScalarGridSpec(
            num_scalar_prefetch=1,
            grid=(steps,),
            in_specs=[wind_spec] + specs,
            out_specs=[pl.BlockSpec((blocks, TILE_M, LANES), lambda i, sc: (0, i, 0))] * GROUPS,
            scratch_shapes=[
                pltpu.VMEM((2, rows, TILE_M, WIDTH), F32),
                pltpu.VMEM((2, rows, TILE_M, WIDTH), F32),
                pltpu.VMEM((rows, 10, 8, WIDTH), F32),
                pltpu.VMEM((BLOCKS + 2, TILE_M, LANES), F32),
                pltpu.VMEM((GROUPS, TILE_M, LANES), F32),
            ],
        ),
        out_shape=[jax.ShapeDtypeStruct((blocks, MINE, LANES), BF)] * GROUPS,
        compiler_params=pltpu.CompilerParams(vmem_limit_bytes=VMEM),
        cost_estimate=pl.CostEstimate(
            flops=10**7, bytes_accessed=work * 10 * 2**20, transcendentals=0
        ),
        name="observe_inner" if inner else "observe_outer",
    )(scalars, winds, *operands)


def weights_kernel(sc, index, precision, values, spread, pull):
    me, grid_at = sc[0], sc[1]
    patch = me * OWN_PATCHES + pl.program_id(0)
    row_low = grid_at * ROWS - HALO_R
    chunk = 512
    total = jnp.zeros((6 * 32, LANES), F32)
    for c in range(K // chunk):
        at = slice(c * chunk, (c + 1) * chunk)
        cell = index[0, :, at]
        row = lax.shift_right_logical(cell, 10) - row_low
        spot = cell & (LANES - 1)
        weight = precision[0, :, at]
        parts = []
        for item in (weight, weight * values[0, :, at]):
            for _ in range(3):
                top = item.astype(BF).astype(F32)
                parts.append(top)
                item = item - top
        in_row = lax.broadcasted_iota(jnp.int32, (32, chunk), 0) == row
        at_spot = lax.broadcasted_iota(jnp.int32, (LANES, chunk), 0) == spot
        left = jnp.concatenate([jnp.where(in_row, part, 0.0) for part in parts], axis=0).astype(BF)
        right = jnp.where(at_spot, 1.0, 0.0).astype(BF)
        total = total + lax.dot_general(
            left, right, (((1,), (1,)), ((), ())), preferred_element_type=F32
        )
    weight_sum = total[0:32] + total[32:64] + total[64:96]
    value_sum = total[96:128] + total[128:160] + total[160:192]
    r = lax.broadcasted_iota(jnp.int32, (32, LANES), 0).astype(F32)
    offset = (lane_iota(32) - patch * PATCH_C + HALO_R) & (LANES - 1)
    row_diff = r - (HALO_R + (ROWS - 1) * 0.5)
    col_diff = offset.astype(F32) - (HALO_R + (PATCH_C - 1) * 0.5)
    distance = row_diff * row_diff + col_diff * col_diff
    share = jnp.exp(-distance / LOC_AREA) / (MEMBERS - 1.0)
    weight_all = weight_sum * share
    root = jnp.sqrt(weight_all)
    seen = weight_all > 0.0
    spread[0] = root
    pull[0] = jnp.where(seen, value_sum * share / jnp.where(seen, root, 1.0), 0.0)


def weigh(scalars, index, precision, values):
    spec = pl.BlockSpec((1, 1, K), lambda p, sc: (p, 0, 0))
    out = pl.BlockSpec((1, 32, LANES), lambda p, sc: (p, 0, 0))
    shape = jax.ShapeDtypeStruct((OWN_PATCHES, 32, LANES), F32)
    spread, pull = pl.pallas_call(
        weights_kernel,
        grid_spec=pltpu.PrefetchScalarGridSpec(
            num_scalar_prefetch=1,
            grid=(OWN_PATCHES,),
            in_specs=[spec] * 3,
            out_specs=[out] * 2,
        ),
        out_shape=[shape] * 2,
        compiler_params=pltpu.CompilerParams(vmem_limit_bytes=VMEM),
        cost_estimate=pl.CostEstimate(flops=10**9, bytes_accessed=2**18, transcendentals=0),
        name="weigh",
    )(
        scalars,
        index.reshape(OWN_PATCHES, 1, K),
        precision.reshape(OWN_PATCHES, 1, K),
        values.reshape(OWN_PATCHES, 1, K),
    )
    return spread, pull


def own_plan():
    return [
        [(half * INNER + 2 * t, half * INNER + 12, t, 10 + 6 * half + t) for t in range(6)]
        for half in range(2)
    ]


def inner_plan():
    return [
        [(2 * t, 12, t, t) for t in range(6)],
        [(INNER + 2 * t, INNER + 12, t, 26 + t) for t in range(6)],
    ]


def outer_plan():
    rows = [(2 * t, 4, t, 8 + t) for t in range(2)]
    rows += [(5 + 2 * t, 4, 2 + t, 22 + t) for t in range(2)]
    halo = [(10 + 2 * t, 9, 2 + t, 6 + t) for t in range(2)]
    halo += [(14 + 2 * t, 18, t, 24 + t) for t in range(2)]
    return [rows, halo]


def gram_rows(plan, patches, spread, pull, cells, scaled, mean_of, total):
    lane_row = lane_iota(1)
    lane = lane_iota(MINE)
    at_top = lax.broadcasted_iota(jnp.int32, (16, LANES), 0) == 0

    def pick(p, first, second, outer, lanes):
        low_edge = lanes < HALO_R
        high_edge = lanes >= LANES - HALO_R
        if p == 0:
            return jnp.where(high_edge, outer, first)
        if p == 1:
            return jnp.where(low_edge, second, first)
        if p == 2:
            return jnp.where(high_edge, first, second)
        return jnp.where(low_edge, outer, second)

    ones = jnp.full((8, MEMBERS), 1.0, BF)
    used = set()
    for chunk in plan:
        for at, edge_at, _, _ in chunk:
            used |= {at, at + 1, edge_at}
    for at in sorted(used):
        summed = jnp.dot(
            ones, cells[at].reshape(MEMBERS, LANES), preferred_element_type=F32
        )
        mean_of[at] = summed / MEMBERS

    def multiply(c, i, width):
        total[i] = total[i] + lax.dot_general(
            scaled[c, i, :, 0:width],
            scaled[c, i, 0:MEMBERS, 0:width],
            (((1,), (1,)), ((), ())),
            preferred_element_type=F32,
        )

    waiting = []
    for c, chunk in enumerate(plan):
        for n, (at, edge_at, slot, window_row) in enumerate(chunk):
            back = LANES - HALO_R - 2 * HALO_R * slot
            outer_mean = pltpu.roll(mean_of[edge_at], back, 1)[0:1]
            first_mean, second_mean = mean_of[at, 0:1, :], mean_of[at + 1, 0:1, :]
            place = slice(n * LANES, (n + 1) * LANES)
            means, roots = [], []
            for i, p in enumerate(patches):
                mean = pick(p, first_mean, second_mean, outer_mean, lane_row)
                root = spread[p, window_row : window_row + 1, :]
                innov = pull[p, window_row : window_row + 1, :] - root * mean
                scaled[c, i, MEMBERS : MEMBERS + 16, place] = jnp.where(at_top, innov, 0.0).astype(BF)
                means.append(mean)
                roots.append(root)
            for group in range(GROUPS):
                first = cells[at, group].astype(F32)
                second = cells[at + 1, group].astype(F32)
                outer = pltpu.roll(cells[edge_at, group].astype(F32), back, 1)
                for i, p in enumerate(patches):
                    picked = pick(p, first, second, outer, lane)
                    scaled[c, i, group * MINE : (group + 1) * MINE, place] = (
                        (picked - means[i]) * roots[i]
                    ).astype(BF)
            if waiting:
                multiply(*waiting.pop(0))
        for ready in waiting:
            multiply(*ready)
        waiting = [(c, i, len(chunk) * LANES) for i in range(len(patches))]
    for ready in waiting:
        multiply(*ready)


def fetch_all(moves, cells, sems):
    copies = []
    for n, (src, at, count, group) in enumerate(moves):
        copy = pltpu.make_async_copy(src, cells.at[pl.ds(at, count), group], sems.at[n])
        copy.start()
        copies.append(copy)
    for copy in copies:
        copy.wait()


def own_kernel(sc, spread, pull, *refs):
    pieces, totals = refs[0:4], refs[4:6]
    cells, scaled, mean_of, total, sems = refs[6:]
    me = sc[0]
    fetch_all([(pieces[s], 0, 2 * INNER, me ^ s) for s in range(GROUPS)], cells, sems)
    total[...] = jnp.zeros_like(total)
    gram_rows(own_plan(), list(range(OWN_PATCHES)), spread, pull, cells, scaled, mean_of, total)
    for i in range(OWN_PATCHES):
        totals[i // PAIR][i % PAIR] = total[i]


def inner_kernel(sc, spread, pull, *refs):
    before, near, far, totals = refs[0:2], refs[2:4], refs[4:6], refs[6:8]
    cells, scaled, mean_of, total, sems = refs[8:]
    me = sc[0]
    moves = []
    for side in range(2):
        for s in range(GROUPS):
            moves.append(((near, far)[s // 2][side].at[s % 2], side * INNER, INNER, me ^ s))
    fetch_all(moves, cells, sems)
    for i in range(OWN_PATCHES):
        total[i] = before[i // PAIR][i % PAIR]
    gram_rows(inner_plan(), list(range(OWN_PATCHES)), spread, pull, cells, scaled, mean_of, total)
    for i in range(OWN_PATCHES):
        totals[i // PAIR][i % PAIR] = total[i]


def running_gram(kernel, name, scalars, spread, pull, before, pieces):
    vmem = pl.BlockSpec(memory_space=pltpu.VMEM)
    anywhere = pl.BlockSpec(memory_space=pl.ANY)
    return pl.pallas_call(
        kernel,
        in_specs=[pl.BlockSpec(memory_space=pltpu.SMEM)]
        + [vmem] * (2 + len(before))
        + [anywhere] * len(pieces),
        out_specs=[vmem] * 2,
        out_shape=[jax.ShapeDtypeStruct((PAIR, MEMBERS + 16, MEMBERS), F32)] * 2,
        scratch_shapes=[
            pltpu.VMEM((2 * INNER, GROUPS, MINE, LANES), BF),
            pltpu.VMEM((2, OWN_PATCHES, MEMBERS + 16, 6 * LANES), BF),
            pltpu.VMEM((2 * INNER, 8, LANES), F32),
            pltpu.VMEM((OWN_PATCHES, MEMBERS + 16, MEMBERS), F32),
            pltpu.SemaphoreType.DMA((8,)),
        ],
        compiler_params=pltpu.CompilerParams(vmem_limit_bytes=VMEM),
        cost_estimate=pl.CostEstimate(flops=10**7, bytes_accessed=35 * 2**20, transcendentals=0),
        name=name,
    )(scalars, spread, pull, *before, *pieces)


def last_kernel(patches, sc, spread, pull, before, *refs):
    own, low, high, outs = refs[0:4], refs[4], refs[5], refs[6:10]
    cells, scaled, mean_of, total, sems = refs[10:]
    me = sc[0]
    moves = []
    for s in range(GROUPS):
        moves.append((own[s].at[pl.ds(0, 9)], 0, 9, me ^ s))
        moves.append((low.at[s], 9, OUTER, me ^ s))
        moves.append((high.at[s], 14, OUTER, me ^ s))
    fetch_all(moves, cells, sems)
    total[...] = before[...]
    gram_rows(outer_plan(), patches, spread, pull, cells, scaled, mean_of, total)
    for i in range(PAIR):
        for s in range(GROUPS):
            at = pl.multiple_of((me ^ s) * MINE, MINE)
            projected = total[i, MEMBERS : MEMBERS + 8, pl.ds(at, MINE)]
            top = projected.astype(BF).astype(F32)
            zero = jnp.zeros_like(top)
            extra = jnp.concatenate([top, projected - top, zero, zero], axis=1)
            block = total[i, pl.ds(at, MINE), :]
            if s == 0:
                outs[s][i, 0:MINE, :] = block
                outs[s][i, MINE : MINE + 8, :] = extra
            else:
                outs[s][i, 0:MINE, :] = block.astype(BF)
                outs[s][i, MINE : MINE + 16, :] = jnp.concatenate([extra, extra], axis=0).astype(BF)


def last_gram(patches, scalars, spread, pull, before, own, low, high):
    vmem = pl.BlockSpec(memory_space=pltpu.VMEM)
    anywhere = pl.BlockSpec(memory_space=pl.ANY)
    return pl.pallas_call(
        functools.partial(last_kernel, patches),
        in_specs=[pl.BlockSpec(memory_space=pltpu.SMEM), vmem, vmem, vmem] + [anywhere] * 6,
        out_specs=[vmem] * GROUPS,
        out_shape=[jax.ShapeDtypeStruct((PAIR, MINE + 8, MEMBERS), F32)]
        + [jax.ShapeDtypeStruct((PAIR, MINE + 16, MEMBERS), BF)] * (GROUPS - 1),
        scratch_shapes=[
            pltpu.VMEM((19, GROUPS, MINE, LANES), BF),
            pltpu.VMEM((2, PAIR, MEMBERS + 16, 4 * LANES), BF),
            pltpu.VMEM((19, 8, LANES), F32),
            pltpu.VMEM((PAIR, MEMBERS + 16, MEMBERS), F32),
            pltpu.SemaphoreType.DMA((12,)),
        ],
        compiler_params=pltpu.CompilerParams(vmem_limit_bytes=VMEM),
        cost_estimate=pl.CostEstimate(flops=10**7, bytes_accessed=30 * 2**20, transcendentals=0),
        name=f"gram_last_{patches[0]}",
    )(scalars, spread, pull, before, *own, low, high)


def assemble_kernel(which, sc, *refs):
    gram, proj = refs[-2], refs[-1]
    for n, s in enumerate(which):

        @pl.when(pl.program_id(0) == n)
        def _(n=n, s=s):
            for p in range(PAIR):
                gram[p] = refs[n][p, 0:MINE, :].astype(F32)
                extra = refs[n][p, MINE : MINE + (8 if s == 0 else 16), :].astype(F32)
                proj[0, p : p + 1, :] = extra[0:1, 0:MINE] + extra[0:1, MINE : 2 * MINE]


def assemble(half, which, scalars, parts, begun):
    def at(n, sc):
        return ((sc[0] ^ (n + which[0])) * 2 + half, 0, 0)

    begun = [] if begun is None else list(begun)
    count = len(which)
    return pl.pallas_call(
        functools.partial(assemble_kernel, which),
        grid_spec=pltpu.PrefetchScalarGridSpec(
            num_scalar_prefetch=1,
            grid=(count,),
            in_specs=[pl.BlockSpec(parts[s].shape, lambda n, sc: (0, 0, 0)) for s in which]
            + [pl.BlockSpec(memory_space=pl.ANY)] * len(begun),
            out_specs=[
                pl.BlockSpec((PAIR, MINE, MEMBERS), at),
                pl.BlockSpec((1, PAIR, MINE), at),
            ],
        ),
        out_shape=[
            jax.ShapeDtypeStruct((GROUPS * OWN_PATCHES, MINE, MEMBERS), F32),
            jax.ShapeDtypeStruct((2 * GROUPS, PAIR, MINE), F32),
        ],
        input_output_aliases={count + 1: 0, count + 2: 1} if begun else {},
        compiler_params=pltpu.CompilerParams(vmem_limit_bytes=VMEM),
        cost_estimate=pl.CostEstimate(flops=10**6, bytes_accessed=count * 2**20, transcendentals=0),
        name=f"assemble_{half}_{which[0]}",
    )(scalars, *[parts[s] for s in which], *begun)


def bundle_kernel(plan, count, arrays, *refs):
    sources, outs, sems = refs[:arrays], refs[arrays : arrays + 2], refs[arrays + 2]
    copies = []
    for out, starts in zip(outs, plan):
        for k, start in enumerate(starts):
            source = sources[k].at[pl.ds(start, count)]
            copies.append(pltpu.make_async_copy(source, out.at[k], sems.at[len(copies)]))
    for copy in copies:
        copy.start()
    for copy in copies:
        copy.wait()


def bundle(name, pieces, count, low_start, high_start):
    n = len(pieces)
    plan = ([low_start] * n, [high_start] * n)
    anywhere = pl.BlockSpec(memory_space=pl.ANY)
    return pl.pallas_call(
        functools.partial(bundle_kernel, plan, count, n),
        in_specs=[anywhere] * n,
        out_specs=[pl.BlockSpec(memory_space=pltpu.VMEM)] * 2,
        out_shape=[jax.ShapeDtypeStruct((n, count, MINE, LANES), BF)] * 2,
        scratch_shapes=[pltpu.SemaphoreType.DMA((2 * n,))],
        compiler_params=pltpu.CompilerParams(vmem_limit_bytes=VMEM),
        cost_estimate=pl.CostEstimate(flops=0, bytes_accessed=4 * 2**20, transcendentals=0),
        name=name,
    )(*pieces)


def after(*arrays):
    return lax.optimization_barrier(arrays)


def per_device(field, winds, obs_index, measured_values, precision_weights):
    grid_size = lax.axis_size("grid")
    me = lax.axis_index("mem")
    scalars = jnp.stack([me, lax.axis_index("grid")]).astype(jnp.int32)
    forward = [(i, i + 1) for i in range(grid_size - 1)]
    backward = [(i + 1, i) for i in range(grid_size - 1)]

    def swap(x, s):
        return lax.ppermute(x, "mem", [(i, i ^ s) for i in range(GROUPS)])

    def exchange(pieces):
        far = [swap(pieces[s], s) for s in (2, 3)]
        return [pieces[0], swap(pieces[1], 1)] + far

    top, bottom = edges(winds, field)
    low = lax.ppermute(bottom, "grid", forward)
    high = lax.ppermute(top, "grid", backward)

    inner = observe(True, scalars, winds, field)
    low, high, *inner = after(low, high, *inner)
    far_inner = [swap(inner[s], s) for s in (2, 3)]
    near_inner = [inner[0], swap(inner[1], 1)]
    near_up, near_down = bundle("bundle_near", near_inner, INNER, INNER, 0)
    near_up, near_down, low, obs_index, measured_values, precision_weights = after(
        near_up, near_down, low, obs_index, measured_values, precision_weights
    )
    near_low = lax.ppermute(near_up, "grid", forward)
    near_high = lax.ppermute(near_down, "grid", backward)

    outer = observe(False, scalars, winds, field, low, high)

    def mine(x):
        return lax.dynamic_slice_in_dim(x, me * OWN_PATCHES, OWN_PATCHES, 0)

    spread, pull = weigh(scalars, mine(obs_index), mine(precision_weights), mine(measured_values))

    far_inner[0], far_inner[1], spread, pull, *outer = after(*far_inner, spread, pull, *outer)
    far_up, far_down = bundle("bundle_far", far_inner, INNER, INNER, 0)
    totals = running_gram(
        own_kernel, "gram_own", scalars, spread, pull, [], near_inner + far_inner
    )
    near_low, near_high, far_up, far_down, *rest = after(
        near_low, near_high, far_up, far_down, *totals, *outer
    )
    totals, outer = rest[:2], rest[2:]
    far_outer = [swap(outer[s], s) for s in (2, 3)]
    far_up, far_down, core_outer = after(far_up, far_down, swap(outer[1], 1))
    outer = [outer[0], core_outer] + far_outer
    far_low = lax.ppermute(far_up, "grid", forward)
    far_high = lax.ppermute(far_down, "grid", backward)
    outer_up, outer_down = bundle("bundle_outer", outer, OUTER, 4, 0)
    outer_low = lax.ppermute(outer_up, "grid", forward)
    outer_high = lax.ppermute(outer_down, "grid", backward)

    halos = [near_low, near_high, far_low, far_high]
    totals = running_gram(
        inner_kernel, "gram_inner", scalars, spread, pull, totals, halos
    )
    result = None
    for n in range(2):
        patches = [PAIR * n, PAIR * n + 1]
        sent = last_gram(
            patches, scalars, spread, pull, totals[n], outer, outer_low, outer_high
        )
        parts = exchange(sent)
        for which in ([0, 1, 2, 3],) if n == 0 else ([0, 1], [2], [3]):
            result = assemble(n, which, scalars, parts, result)
    return result[0], result[1].reshape(GROUPS * OWN_PATCHES, MINE)


def solution(mesh):
    return jax.shard_map(
        per_device,
        mesh=mesh,
        in_specs=(
            P("mem", None, "grid", None),
            P(None, None, "grid", None),
            P("grid", None),
            P("grid", None),
            P("grid", None),
        ),
        out_specs=(P("grid", "mem", None), P("grid", "mem")),
        check_vma=False,
    )
```

```python
import functools

import jax
import jax.numpy as jnp
from jax import lax
from jax.experimental import pallas as pl
from jax.experimental.pallas import tpu as pltpu
from jax.sharding import PartitionSpec as P

PATCH_C = 64
HALO_R = 8
LOC_AREA = 512.0
LOW_SHARE = 0.7
HIGH_SHARE = 0.3

ROWS = 16
WIDTH = 1024
MINE = 128
GROUPS = 4
MEMBERS = MINE * GROUPS
LANES = 128
BLOCKS = WIDTH // LANES
TILE_M = 64
INNER = 13
OUTER = 5
OWN_PATCHES = 4
K = 3072
PAIR = 2
VMEM = 60 * 1024 * 1024
BF = jnp.bfloat16
F32 = jnp.float32


def lane_iota(rows):
    return lax.broadcasted_iota(jnp.int32, (rows, LANES), 1)


def row_choice(picked, row_of):
    shape = (picked * 16, 16 * ROWS)
    out = lax.broadcasted_iota(jnp.int32, shape, 0)
    source = (out & 15) * ROWS + row_of(lax.shift_right_logical(out, 4))
    return jnp.where(source == lax.broadcasted_iota(jnp.int32, shape, 1), 1.0, 0.0).astype(BF)


def choose_rows(choice, field, start, level):
    members = field[pl.ds(start, 16), level].reshape(16 * ROWS, WIDTH)
    return jnp.dot(choice, members, preferred_element_type=F32)


def edges_kernel(wind, field, top, bottom):
    step = pl.program_id(0)
    choice = row_choice(4, lambda r: jnp.where(r < 2, r, r + ROWS - 4))

    @pl.when(step == 0)
    def _():
        for pack, row in ((top, 0), (bottom, ROWS - 1)):
            winds = [
                wind[part, level].astype(F32)[row : row + 1] for part in range(2) for level in range(2)
            ]
            rows = jnp.concatenate(winds + [jnp.zeros((12, WIDTH), F32)], axis=0)
            pack[4 * MINE : 4 * MINE + 16] = rows.astype(BF)

    for group in range(TILE_M // 16):
        for level in range(2):
            rows = choose_rows(choice, field, group * 16, level).astype(BF)
            for i in range(2):
                at = pl.multiple_of((level * 2 + i) * MINE + step * TILE_M + group * 16, 16)
                top[pl.ds(at, 16)] = rows[i * 16 : (i + 1) * 16]
                bottom[pl.ds(at, 16)] = rows[32 + i * 16 : 48 + i * 16]


def edges(winds, field):
    pack = jax.ShapeDtypeStruct((4 * MINE + 16, WIDTH), BF)
    return pl.pallas_call(
        edges_kernel,
        grid=(MINE // TILE_M,),
        in_specs=[
            pl.BlockSpec((2, 2, ROWS, WIDTH), lambda i: (0, 0, 0, 0)),
            pl.BlockSpec((TILE_M, 2, ROWS, WIDTH), lambda i: (i, 0, 0, 0)),
        ],
        out_specs=[pl.BlockSpec(pack.shape, lambda i: (0, 0))] * 2,
        out_shape=[pack] * 2,
        compiler_params=pltpu.CompilerParams(vmem_limit_bytes=VMEM),
        cost_estimate=pl.CostEstimate(flops=10**7, bytes_accessed=10 * 2**20, transcendentals=0),
        name="edges",
    )(winds, field)


def observe_kernel(inner, sc, wind, field, *refs):
    if inner:
        rows = ROWS
    else:
        lows, low_wind = refs[0:4], refs[4]
        highs, high_wind = refs[5:9], refs[9]
        refs = refs[10:]
        rows = 12
    outs = refs[0:4]
    raw, once, coef, row_out, edge = refs[4:]
    me = sc[0]
    lane = lane_iota(TILE_M)
    first = lane_iota(8) == 0
    last = lane_iota(8) == LANES - 1

    @pl.when(pl.program_id(0) == 0)
    def _():
        column = lax.broadcasted_iota(jnp.int32, (1, WIDTH), 1)

        def coefs(a, b):
            up, down = jnp.maximum(a, 0.0), -jnp.minimum(a, 0.0)
            left, right = jnp.maximum(b, 0.0), -jnp.minimum(b, 0.0)
            centre = 1.0 - up - down - left - right
            left = jnp.where(column == 0, 0.0, left)
            right = jnp.where(column == WIDTH - 1, 0.0, right)
            return centre, up, down, left, right

        def put(at_row, level, arrays, r):
            for k, array in enumerate(arrays):
                coef[at_row, level * 5 + k] = jnp.broadcast_to(array[r : r + 1], (8, WIDTH))

        if inner:
            places = [(r, r) for r in range(1, ROWS - 1)]
        else:
            places = [(2, 0), (3, 1), (4, 2), (7, 13), (8, 14), (9, 15)]
        for level in range(2):
            arrays = coefs(wind[0, level].astype(F32), wind[1, level].astype(F32))
            for at_row, r in places:
                put(at_row, level, arrays, r)
            if not inner:
                for side, at_row in ((low_wind, 1), (high_wind, 10)):
                    winds = side[...].astype(F32)
                    put(at_row, level, coefs(winds[level : level + 1], winds[2 + level : 3 + level]), 0)
        row_out[0] = jnp.zeros((TILE_M, LANES), F32)
        row_out[BLOCKS + 1] = jnp.zeros((TILE_M, LANES), F32)

    if inner:
        picked, at_first, choice = ROWS, 0, row_choice(ROWS, lambda r: r)
    else:
        picked, at_first, choice = 8, 2, row_choice(8, lambda r: jnp.where(r < 4, r, r + 8))
        for level in range(2):
            for i in range(2):
                raw[level, i] = lows[level * 2 + i][...].astype(F32)
                raw[level, 10 + i] = highs[level * 2 + i][...].astype(F32)

    def reorder(group, carry):
        start = pl.multiple_of(group * 16, 16)
        for level in range(2):
            chosen = choose_rows(choice, field, start, level)
            for r in range(picked):
                raw[level, at_first + r, pl.ds(start, 16), :] = chosen[r * 16 : (r + 1) * 16]
        return carry

    lax.fori_loop(0, TILE_M // 16, reorder, 0)

    def stencil(src, level, row):
        tiles = range(TILE_M // 8)

        def block(at_row, m, j):
            return src[level, at_row, m * 8 : (m + 1) * 8, j * LANES : (j + 1) * LANES]

        here = [block(row, m, 0) for m in tiles]
        before = [None for m in tiles]
        turned_back = [pltpu.roll(here[m], LANES - 1, 1) for m in tiles]
        for j in range(BLOCKS):
            lanes = slice(j * LANES, (j + 1) * LANES)
            centre, up, down, west, east = (coef[row, level * 5 + k, :, lanes] for k in range(5))
            for m in tiles:
                turned = pltpu.roll(here[m], 1, 1)
                left = turned if j == 0 else jnp.where(first, before[m], turned)
                right = turned_back[m]
                after, after_back = None, None
                if j + 1 < BLOCKS:
                    after = block(row, m, j + 1)
                    after_back = pltpu.roll(after, LANES - 1, 1)
                    right = jnp.where(last, after_back, right)
                value = (
                    centre * here[m]
                    + up * block(row - 1, m, j)
                    + down * block(row + 1, m, j)
                    + west * left
                    + east * right
                )
                yield j, slice(m * 8, (m + 1) * 8), value
                before[m], here[m], turned_back[m] = turned, after, after_back

    def step_one(row, carry):
        for level in range(2):
            for j, members, value in stencil(raw, level, row):
                once[level, row, members, j * LANES : (j + 1) * LANES] = value
        return carry

    def step_two(row, base, slot):
        for j, members, value in stencil(once, 0, row):
            row_out[1 + j, members] = LOW_SHARE * value
        for j, members, value in stencil(once, 1, row):
            row_out[1 + j, members] = row_out[1 + j, members] + HIGH_SHARE * value
        for s in range(GROUPS):
            d = me ^ s
            for j in range(2):
                outs[s][base + j] = row_out[1 + 2 * d + j].astype(BF)
            outer = jnp.where(
                lane < HALO_R,
                row_out[2 * d + 3],
                jnp.where(lane >= LANES - HALO_R, row_out[2 * d], 0.0),
            )
            edge[s] = edge[s] + pltpu.roll(outer, HALO_R + 2 * HALO_R * slot, 1)

    def clear():
        for s in range(GROUPS):
            edge[s] = jnp.zeros((TILE_M, LANES), F32)

    def flush(at):
        for s in range(GROUPS):
            outs[s][at] = edge[s].astype(BF)

    if inner:
        lax.fori_loop(1, ROWS - 1, step_one, 0)
        for half in range(2):
            clear()

            def step(t, carry, half=half):
                step_two(2 + half * 6 + t, half * INNER + 2 * t, t)
                return carry

            lax.fori_loop(0, 6, step, 0)
            flush(half * INNER + 12)
    else:
        lax.fori_loop(1, 5, step_one, 0)
        lax.fori_loop(7, 11, step_one, 0)
        clear()

        def step(t, carry):
            under = t // 2
            step_two(2 + t + 4 * under, 2 * t + under, t)
            return carry

        lax.fori_loop(0, 4, step, 0)
        flush(4)


def observe(inner, scalars, winds, *arrays):
    steps = MINE // TILE_M
    wind_spec = pl.BlockSpec((2, 2, ROWS, WIDTH), lambda i, sc: (0, 0, 0, 0))
    specs = [pl.BlockSpec((TILE_M, 2, ROWS, WIDTH), lambda i, sc: (i, 0, 0, 0))]
    if inner:
        rows, blocks, work = ROWS, 2 * INNER, 7
        operands = arrays
    else:
        rows, blocks, work = 12, 9, 3
        side = [
            pl.BlockSpec((TILE_M, WIDTH), functools.partial(lambda k, i, sc: (k * steps + i, 0), k))
            for k in range(4)
        ] + [pl.BlockSpec((16, WIDTH), lambda i, sc: (4 * MINE // 16, 0))]
        specs = specs + side * 2
        field, low, high = arrays
        operands = [field] + [low] * 5 + [high] * 5
    return pl.pallas_call(
        functools.partial(observe_kernel, inner),
        grid_spec=pltpu.PrefetchScalarGridSpec(
            num_scalar_prefetch=1,
            grid=(steps,),
            in_specs=[wind_spec] + specs,
            out_specs=[pl.BlockSpec((blocks, TILE_M, LANES), lambda i, sc: (0, i, 0))] * GROUPS,
            scratch_shapes=[
                pltpu.VMEM((2, rows, TILE_M, WIDTH), F32),
                pltpu.VMEM((2, rows, TILE_M, WIDTH), F32),
                pltpu.VMEM((rows, 10, 8, WIDTH), F32),
                pltpu.VMEM((BLOCKS + 2, TILE_M, LANES), F32),
                pltpu.VMEM((GROUPS, TILE_M, LANES), F32),
            ],
        ),
        out_shape=[jax.ShapeDtypeStruct((blocks, MINE, LANES), BF)] * GROUPS,
        compiler_params=pltpu.CompilerParams(vmem_limit_bytes=VMEM),
        cost_estimate=pl.CostEstimate(
            flops=10**7, bytes_accessed=work * 10 * 2**20, transcendentals=0
        ),
        name="observe_inner" if inner else "observe_outer",
    )(scalars, winds, *operands)


def weights_kernel(sc, index, precision, values, spread, pull):
    me, grid_at = sc[0], sc[1]
    patch = me * OWN_PATCHES + pl.program_id(0)
    row_low = grid_at * ROWS - HALO_R
    chunk = 512
    total = jnp.zeros((6 * 32, LANES), F32)
    for c in range(K // chunk):
        at = slice(c * chunk, (c + 1) * chunk)
        cell = index[0, :, at]
        row = lax.shift_right_logical(cell, 10) - row_low
        spot = cell & (LANES - 1)
        weight = precision[0, :, at]
        parts = []
        for item in (weight, weight * values[0, :, at]):
            for _ in range(3):
                top = item.astype(BF).astype(F32)
                parts.append(top)
                item = item - top
        in_row = lax.broadcasted_iota(jnp.int32, (32, chunk), 0) == row
        at_spot = lax.broadcasted_iota(jnp.int32, (LANES, chunk), 0) == spot
        left = jnp.concatenate([jnp.where(in_row, part, 0.0) for part in parts], axis=0).astype(BF)
        right = jnp.where(at_spot, 1.0, 0.0).astype(BF)
        total = total + lax.dot_general(
            left, right, (((1,), (1,)), ((), ())), preferred_element_type=F32
        )
    weight_sum = total[0:32] + total[32:64] + total[64:96]
    value_sum = total[96:128] + total[128:160] + total[160:192]
    r = lax.broadcasted_iota(jnp.int32, (32, LANES), 0).astype(F32)
    offset = (lane_iota(32) - patch * PATCH_C + HALO_R) & (LANES - 1)
    row_diff = r - (HALO_R + (ROWS - 1) * 0.5)
    col_diff = offset.astype(F32) - (HALO_R + (PATCH_C - 1) * 0.5)
    distance = row_diff * row_diff + col_diff * col_diff
    share = jnp.exp(-distance / LOC_AREA) / (MEMBERS - 1.0)
    weight_all = weight_sum * share
    root = jnp.sqrt(weight_all)
    seen = weight_all > 0.0
    spread[0] = root
    pull[0] = jnp.where(seen, value_sum * share / jnp.where(seen, root, 1.0), 0.0)


def weigh(scalars, index, precision, values):
    spec = pl.BlockSpec((1, 1, K), lambda p, sc: (p, 0, 0))
    out = pl.BlockSpec((1, 32, LANES), lambda p, sc: (p, 0, 0))
    shape = jax.ShapeDtypeStruct((OWN_PATCHES, 32, LANES), F32)
    spread, pull = pl.pallas_call(
        weights_kernel,
        grid_spec=pltpu.PrefetchScalarGridSpec(
            num_scalar_prefetch=1,
            grid=(OWN_PATCHES,),
            in_specs=[spec] * 3,
            out_specs=[out] * 2,
        ),
        out_shape=[shape] * 2,
        compiler_params=pltpu.CompilerParams(vmem_limit_bytes=VMEM),
        cost_estimate=pl.CostEstimate(flops=10**9, bytes_accessed=2**18, transcendentals=0),
        name="weigh",
    )(
        scalars,
        index.reshape(OWN_PATCHES, 1, K),
        precision.reshape(OWN_PATCHES, 1, K),
        values.reshape(OWN_PATCHES, 1, K),
    )
    return spread, pull


def own_plan():
    return [
        [(half * INNER + 2 * t, half * INNER + 12, t, 10 + 6 * half + t) for t in range(6)]
        for half in range(2)
    ]


def inner_plan():
    low = [(2 * t, 12, t, t) for t in range(6)]
    high = [(INNER + 2 * t, INNER + 12, t, 26 + t) for t in range(6)]
    at = 2 * INNER
    outer = [(at + 2 * t, at + 4, t, 8 + t) for t in range(2)]
    outer += [(at + 5 + 2 * t, at + 4, 2 + t, 22 + t) for t in range(2)]
    return [low, high, outer]


def outer_plan():
    rows = [(1 + 2 * t, 0, 2 + t, 6 + t) for t in range(2)]
    rows += [(OUTER + 2 * t, OUTER + 4, t, 24 + t) for t in range(2)]
    return [rows]


def gram_rows(plan, patches, spread, pull, cells, scaled, mean_of, total):
    lane_row = lane_iota(1)
    lane = lane_iota(MINE)
    at_top = lax.broadcasted_iota(jnp.int32, (16, LANES), 0) == 0

    def pick(p, first, second, outer, lanes):
        low_edge = lanes < HALO_R
        high_edge = lanes >= LANES - HALO_R
        if p == 0:
            return jnp.where(high_edge, outer, first)
        if p == 1:
            return jnp.where(low_edge, second, first)
        if p == 2:
            return jnp.where(high_edge, first, second)
        return jnp.where(low_edge, outer, second)

    ones = jnp.full((8, MEMBERS), 1.0, BF)
    used = set()
    for chunk in plan:
        for at, edge_at, _, _ in chunk:
            used |= {at, at + 1, edge_at}
    for at in sorted(used):
        summed = jnp.dot(
            ones, cells[at].reshape(MEMBERS, LANES), preferred_element_type=F32
        )
        mean_of[at] = summed / MEMBERS

    def multiply(c, i, width):
        total[i] = total[i] + lax.dot_general(
            scaled[c, i, :, 0:width],
            scaled[c, i, 0:MEMBERS, 0:width],
            (((1,), (1,)), ((), ())),
            preferred_element_type=F32,
        )

    waiting = []
    for c, chunk in enumerate(plan):
        for n, (at, edge_at, slot, window_row) in enumerate(chunk):
            back = LANES - HALO_R - 2 * HALO_R * slot
            outer_mean = pltpu.roll(mean_of[edge_at], back, 1)[0:1]
            first_mean, second_mean = mean_of[at, 0:1, :], mean_of[at + 1, 0:1, :]
            place = slice(n * LANES, (n + 1) * LANES)
            means, roots = [], []
            for i, p in enumerate(patches):
                mean = pick(p, first_mean, second_mean, outer_mean, lane_row)
                root = spread[p, window_row : window_row + 1, :]
                innov = pull[p, window_row : window_row + 1, :] - root * mean
                scaled[c, i, MEMBERS : MEMBERS + 16, place] = jnp.where(at_top, innov, 0.0).astype(BF)
                means.append(mean)
                roots.append(root)
            for group in range(GROUPS):
                first = cells[at, group].astype(F32)
                second = cells[at + 1, group].astype(F32)
                outer = pltpu.roll(cells[edge_at, group].astype(F32), back, 1)
                for i, p in enumerate(patches):
                    picked = pick(p, first, second, outer, lane)
                    scaled[c, i, group * MINE : (group + 1) * MINE, place] = (
                        (picked - means[i]) * roots[i]
                    ).astype(BF)
            if waiting:
                multiply(*waiting.pop(0))
        for ready in waiting:
            multiply(*ready)
        waiting = [(c, i, len(chunk) * LANES) for i in range(len(patches))]
    for ready in waiting:
        multiply(*ready)


def fetch_all(moves, cells, sems):
    copies = []
    for n, (src, at, count, group) in enumerate(moves):
        copy = pltpu.make_async_copy(src, cells.at[pl.ds(at, count), group], sems.at[n])
        copy.start()
        copies.append(copy)
    for copy in copies:
        copy.wait()


def own_kernel(sc, spread, pull, *refs):
    pieces, totals = refs[0:4], refs[4:6]
    cells, scaled, mean_of, total, sems = refs[6:]
    me = sc[0]
    fetch_all([(pieces[s], 0, 2 * INNER, me ^ s) for s in range(GROUPS)], cells, sems)
    total[...] = jnp.zeros_like(total)
    gram_rows(own_plan(), list(range(OWN_PATCHES)), spread, pull, cells, scaled, mean_of, total)
    for i in range(OWN_PATCHES):
        totals[i // PAIR][i % PAIR] = total[i]


def inner_kernel(sc, spread, pull, *refs):
    before, near, far, outer, totals = refs[0:2], refs[2:4], refs[4:6], refs[6:10], refs[10:12]
    cells, scaled, mean_of, total, sems = refs[12:]
    me = sc[0]
    moves = []
    for side in range(2):
        for s in range(GROUPS):
            moves.append(((near, far)[s // 2][side].at[s % 2], side * INNER, INNER, me ^ s))
    for s in range(GROUPS):
        moves.append((outer[s], 2 * INNER, 9, me ^ s))
    fetch_all(moves, cells, sems)
    for i in range(OWN_PATCHES):
        total[i] = before[i // PAIR][i % PAIR]
    gram_rows(inner_plan(), list(range(OWN_PATCHES)), spread, pull, cells, scaled, mean_of, total)
    for i in range(OWN_PATCHES):
        totals[i // PAIR][i % PAIR] = total[i]


def running_gram(kernel, plan, name, scalars, spread, pull, before, pieces):
    vmem = pl.BlockSpec(memory_space=pltpu.VMEM)
    anywhere = pl.BlockSpec(memory_space=pl.ANY)
    blocks = 2 * INNER + 9 * (len(plan) - 2)
    return pl.pallas_call(
        kernel,
        in_specs=[pl.BlockSpec(memory_space=pltpu.SMEM)]
        + [vmem] * (2 + len(before))
        + [anywhere] * len(pieces),
        out_specs=[vmem] * 2,
        out_shape=[jax.ShapeDtypeStruct((PAIR, MEMBERS + 16, MEMBERS), F32)] * 2,
        scratch_shapes=[
            pltpu.VMEM((blocks, GROUPS, MINE, LANES), BF),
            pltpu.VMEM((len(plan), OWN_PATCHES, MEMBERS + 16, 6 * LANES), BF),
            pltpu.VMEM((blocks, 8, LANES), F32),
            pltpu.VMEM((OWN_PATCHES, MEMBERS + 16, MEMBERS), F32),
            pltpu.SemaphoreType.DMA((12,)),
        ],
        compiler_params=pltpu.CompilerParams(vmem_limit_bytes=VMEM),
        cost_estimate=pl.CostEstimate(flops=10**7, bytes_accessed=35 * 2**20, transcendentals=0),
        name=name,
    )(scalars, spread, pull, *before, *pieces)


def last_kernel(patches, sc, spread, pull, before, low, high, *refs):
    outs = refs[0:4]
    cells, scaled, mean_of, total, sems = refs[4:]
    me = sc[0]
    moves = []
    for s in range(GROUPS):
        moves.append((low.at[s], 0, OUTER, me ^ s))
        moves.append((high.at[s], OUTER, OUTER, me ^ s))
    fetch_all(moves, cells, sems)
    total[...] = before[...]
    gram_rows(outer_plan(), patches, spread, pull, cells, scaled, mean_of, total)
    for s in range(GROUPS):
        at = pl.multiple_of((me ^ s) * MINE, MINE)
        extra = []
        for i in range(PAIR):
            projected = total[i, MEMBERS : MEMBERS + 8, pl.ds(at, MINE)]
            top = projected.astype(BF).astype(F32)
            extra += [top, projected - top]
            block = total[i, pl.ds(at, MINE), :]
            outs[s][i * MINE : (i + 1) * MINE, :] = block.astype(outs[s].dtype)
        extra = jnp.concatenate(extra, axis=1)
        if s > 0:
            extra = jnp.concatenate([extra, extra], axis=0).astype(BF)
        outs[s][PAIR * MINE :, :] = extra


def last_gram(patches, scalars, spread, pull, before, low, high):
    vmem = pl.BlockSpec(memory_space=pltpu.VMEM)
    anywhere = pl.BlockSpec(memory_space=pl.ANY)
    rows = PAIR * MINE
    return pl.pallas_call(
        functools.partial(last_kernel, patches),
        in_specs=[pl.BlockSpec(memory_space=pltpu.SMEM), vmem, vmem, vmem] + [anywhere] * 2,
        out_specs=[vmem] * GROUPS,
        out_shape=[jax.ShapeDtypeStruct((rows + 8, MEMBERS), F32)]
        + [jax.ShapeDtypeStruct((rows + 16, MEMBERS), BF)] * (GROUPS - 1),
        scratch_shapes=[
            pltpu.VMEM((2 * OUTER, GROUPS, MINE, LANES), BF),
            pltpu.VMEM((1, PAIR, MEMBERS + 16, 4 * LANES), BF),
            pltpu.VMEM((2 * OUTER, 8, LANES), F32),
            pltpu.VMEM((PAIR, MEMBERS + 16, MEMBERS), F32),
            pltpu.SemaphoreType.DMA((8,)),
        ],
        compiler_params=pltpu.CompilerParams(vmem_limit_bytes=VMEM),
        cost_estimate=pl.CostEstimate(flops=10**7, bytes_accessed=20 * 2**20, transcendentals=0),
        name=f"gram_last_{patches[0]}",
    )(scalars, spread, pull, before, low, high)


def assemble_kernel(which, sc, *refs):
    gram, proj = refs[-2], refs[-1]
    for n, s in enumerate(which):

        @pl.when(pl.program_id(0) == n)
        def _(n=n, s=s):
            for p in range(PAIR):
                gram[p] = refs[n][p * MINE : (p + 1) * MINE, :].astype(F32)
                at = p * 2 * MINE
                extra = refs[n][PAIR * MINE :, at : at + 2 * MINE].astype(F32)
                proj[0, p : p + 1, :] = extra[0:1, 0:MINE] + extra[0:1, MINE:]


def assemble(half, which, scalars, parts, begun):
    def at(n, sc):
        return ((sc[0] ^ (n + which[0])) * 2 + half, 0, 0)

    begun = [] if begun is None else list(begun)
    count = len(which)
    return pl.pallas_call(
        functools.partial(assemble_kernel, which),
        grid_spec=pltpu.PrefetchScalarGridSpec(
            num_scalar_prefetch=1,
            grid=(count,),
            in_specs=[pl.BlockSpec(parts[s].shape, lambda n, sc: (0, 0)) for s in which]
            + [pl.BlockSpec(memory_space=pl.ANY)] * len(begun),
            out_specs=[
                pl.BlockSpec((PAIR, MINE, MEMBERS), at),
                pl.BlockSpec((1, PAIR, MINE), at),
            ],
        ),
        out_shape=[
            jax.ShapeDtypeStruct((GROUPS * OWN_PATCHES, MINE, MEMBERS), F32),
            jax.ShapeDtypeStruct((2 * GROUPS, PAIR, MINE), F32),
        ],
        input_output_aliases={count + 1: 0, count + 2: 1} if begun else {},
        compiler_params=pltpu.CompilerParams(vmem_limit_bytes=VMEM),
        cost_estimate=pl.CostEstimate(flops=10**6, bytes_accessed=count * 2**20, transcendentals=0),
        name=f"assemble_{half}_{which[0]}",
    )(scalars, *[parts[s] for s in which], *begun)


def bundle_kernel(plan, count, arrays, *refs):
    sources, outs, sems = refs[:arrays], refs[arrays : arrays + 2], refs[arrays + 2]
    copies = []
    for out, starts in zip(outs, plan):
        for k, start in enumerate(starts):
            source = sources[k].at[pl.ds(start, count)]
            copies.append(pltpu.make_async_copy(source, out.at[k], sems.at[len(copies)]))
    for copy in copies:
        copy.start()
    for copy in copies:
        copy.wait()


def bundle(name, pieces, count, low_start, high_start):
    n = len(pieces)
    plan = ([low_start] * n, [high_start] * n)
    anywhere = pl.BlockSpec(memory_space=pl.ANY)
    return pl.pallas_call(
        functools.partial(bundle_kernel, plan, count, n),
        in_specs=[anywhere] * n,
        out_specs=[pl.BlockSpec(memory_space=pltpu.VMEM)] * 2,
        out_shape=[jax.ShapeDtypeStruct((n, count, MINE, LANES), BF)] * 2,
        scratch_shapes=[pltpu.SemaphoreType.DMA((2 * n,))],
        compiler_params=pltpu.CompilerParams(vmem_limit_bytes=VMEM),
        cost_estimate=pl.CostEstimate(flops=0, bytes_accessed=4 * 2**20, transcendentals=0),
        name=name,
    )(*pieces)


def after(*arrays):
    return lax.optimization_barrier(arrays)


def per_device(field, winds, obs_index, measured_values, precision_weights):
    grid_size = lax.axis_size("grid")
    me = lax.axis_index("mem")
    scalars = jnp.stack([me, lax.axis_index("grid")]).astype(jnp.int32)
    forward = [(i, i + 1) for i in range(grid_size - 1)]
    backward = [(i + 1, i) for i in range(grid_size - 1)]

    def swap(x, s):
        return lax.ppermute(x, "mem", [(i, i ^ s) for i in range(GROUPS)])

    def exchange(pieces):
        far = [swap(pieces[s], s) for s in (2, 3)]
        return [pieces[0], swap(pieces[1], 1)] + far

    top, bottom = edges(winds, field)
    low = lax.ppermute(bottom, "grid", forward)
    high = lax.ppermute(top, "grid", backward)

    inner = observe(True, scalars, winds, field)
    low, high, *inner = after(low, high, *inner)
    far_inner = [swap(inner[s], s) for s in (2, 3)]
    near_inner = [inner[0], swap(inner[1], 1)]
    near_up, near_down = bundle("bundle_near", near_inner, INNER, INNER, 0)
    near_up, near_down, low, obs_index, measured_values, precision_weights = after(
        near_up, near_down, low, obs_index, measured_values, precision_weights
    )
    near_low = lax.ppermute(near_up, "grid", forward)
    near_high = lax.ppermute(near_down, "grid", backward)

    outer = observe(False, scalars, winds, field, low, high)

    def mine(x):
        return lax.dynamic_slice_in_dim(x, me * OWN_PATCHES, OWN_PATCHES, 0)

    spread, pull = weigh(scalars, mine(obs_index), mine(precision_weights), mine(measured_values))

    far_inner[0], far_inner[1], spread, pull, *outer = after(*far_inner, spread, pull, *outer)
    far_up, far_down = bundle("bundle_far", far_inner, INNER, INNER, 0)
    totals = running_gram(
        own_kernel, own_plan(), "gram_own", scalars, spread, pull, [], near_inner + far_inner
    )
    near_low, near_high, far_up, far_down, *rest = after(
        near_low, near_high, far_up, far_down, *totals, *outer
    )
    totals, outer = rest[:2], rest[2:]
    far_outer = [swap(outer[s], s) for s in (2, 3)]
    far_up, far_down, core_outer = after(far_up, far_down, swap(outer[1], 1))
    outer = [outer[0], core_outer] + far_outer
    far_low = lax.ppermute(far_up, "grid", forward)
    far_high = lax.ppermute(far_down, "grid", backward)
    outer_up, outer_down = bundle("bundle_outer", outer, OUTER, 4, 0)
    outer_low = lax.ppermute(outer_up, "grid", forward)
    outer_high = lax.ppermute(outer_down, "grid", backward)

    halos = [near_low, near_high, far_low, far_high, *outer]
    totals = running_gram(
        inner_kernel, inner_plan(), "gram_inner", scalars, spread, pull, totals, halos
    )
    result = None
    for n in range(2):
        patches = [PAIR * n, PAIR * n + 1]
        sent = last_gram(
            patches, scalars, spread, pull, totals[n], outer_low, outer_high
        )
        parts = exchange(sent)
        for which in ([0, 1, 2, 3],) if n == 0 else ([0, 1], [2], [3]):
            result = assemble(n, which, scalars, parts, result)
    return result[0], result[1].reshape(GROUPS * OWN_PATCHES, MINE)


def solution(mesh):
    return jax.shard_map(
        per_device,
        mesh=mesh,
        in_specs=(
            P("mem", None, "grid", None),
            P(None, None, "grid", None),
            P("grid", None),
            P("grid", None),
            P("grid", None),
        ),
        out_specs=(P("grid", "mem", None), P("grid", "mem")),
        check_vma=False,
    )
```

```python
import functools

import jax
import jax.numpy as jnp
from jax import lax
from jax.experimental import pallas as pl
from jax.experimental.pallas import tpu as pltpu
from jax.sharding import PartitionSpec as P

PATCH_C = 64
HALO_R = 8
LOC_AREA = 512.0
LOW_SHARE = 0.7
HIGH_SHARE = 0.3

ROWS = 16
WIDTH = 1024
MINE = 128
GROUPS = 4
MEMBERS = MINE * GROUPS
LANES = 128
BLOCKS = WIDTH // LANES
TILE_M = 64
INNER = 13
OUTER = 5
OWN_PATCHES = 4
K = 3072
PAIR = 2
VMEM = 60 * 1024 * 1024
BF = jnp.bfloat16
F32 = jnp.float32


def lane_iota(rows):
    return lax.broadcasted_iota(jnp.int32, (rows, LANES), 1)


def row_choice(picked, row_of):
    shape = (picked * 16, 16 * ROWS)
    out = lax.broadcasted_iota(jnp.int32, shape, 0)
    source = (out & 15) * ROWS + row_of(lax.shift_right_logical(out, 4))
    return jnp.where(source == lax.broadcasted_iota(jnp.int32, shape, 1), 1.0, 0.0).astype(BF)


def choose_rows(choice, field, start, level):
    members = field[pl.ds(start, 16), level].reshape(16 * ROWS, WIDTH)
    return jnp.dot(choice, members, preferred_element_type=F32)


def edges_kernel(wind, field, top, bottom):
    step = pl.program_id(0)
    choice = row_choice(4, lambda r: jnp.where(r < 2, r, r + ROWS - 4))

    @pl.when(step == 0)
    def _():
        for pack, row in ((top, 0), (bottom, ROWS - 1)):
            winds = [
                wind[part, level].astype(F32)[row : row + 1] for part in range(2) for level in range(2)
            ]
            rows = jnp.concatenate(winds + [jnp.zeros((12, WIDTH), F32)], axis=0)
            pack[4 * MINE : 4 * MINE + 16] = rows.astype(BF)

    for group in range(TILE_M // 16):
        for level in range(2):
            rows = choose_rows(choice, field, group * 16, level).astype(BF)
            for i in range(2):
                at = pl.multiple_of((level * 2 + i) * MINE + step * TILE_M + group * 16, 16)
                top[pl.ds(at, 16)] = rows[i * 16 : (i + 1) * 16]
                bottom[pl.ds(at, 16)] = rows[32 + i * 16 : 48 + i * 16]


def edges(winds, field):
    pack = jax.ShapeDtypeStruct((4 * MINE + 16, WIDTH), BF)
    return pl.pallas_call(
        edges_kernel,
        grid=(MINE // TILE_M,),
        in_specs=[
            pl.BlockSpec((2, 2, ROWS, WIDTH), lambda i: (0, 0, 0, 0)),
            pl.BlockSpec((TILE_M, 2, ROWS, WIDTH), lambda i: (i, 0, 0, 0)),
        ],
        out_specs=[pl.BlockSpec(pack.shape, lambda i: (0, 0))] * 2,
        out_shape=[pack] * 2,
        compiler_params=pltpu.CompilerParams(vmem_limit_bytes=VMEM),
        cost_estimate=pl.CostEstimate(flops=10**7, bytes_accessed=10 * 2**20, transcendentals=0),
        name="edges",
    )(winds, field)


def observe_kernel(inner, sc, wind, field, *refs):
    if inner:
        rows = ROWS
    else:
        lows, low_wind = refs[0:4], refs[4]
        highs, high_wind = refs[5:9], refs[9]
        refs = refs[10:]
        rows = 12
    outs = refs[0:4]
    raw, once, coef, row_out, edge = refs[4:]
    me = sc[0]
    lane = lane_iota(TILE_M)
    first = lane_iota(8) == 0
    last = lane_iota(8) == LANES - 1

    @pl.when(pl.program_id(0) == 0)
    def _():
        column = lax.broadcasted_iota(jnp.int32, (1, WIDTH), 1)

        def coefs(a, b):
            up, down = jnp.maximum(a, 0.0), -jnp.minimum(a, 0.0)
            left, right = jnp.maximum(b, 0.0), -jnp.minimum(b, 0.0)
            centre = 1.0 - up - down - left - right
            left = jnp.where(column == 0, 0.0, left)
            right = jnp.where(column == WIDTH - 1, 0.0, right)
            return centre, up, down, left, right

        def put(at_row, level, arrays, r):
            for k, array in enumerate(arrays):
                coef[at_row, level * 5 + k] = jnp.broadcast_to(array[r : r + 1], (8, WIDTH))

        if inner:
            places = [(r, r) for r in range(1, ROWS - 1)]
        else:
            places = [(2, 0), (3, 1), (4, 2), (7, 13), (8, 14), (9, 15)]
        for level in range(2):
            arrays = coefs(wind[0, level].astype(F32), wind[1, level].astype(F32))
            for at_row, r in places:
                put(at_row, level, arrays, r)
            if not inner:
                for side, at_row in ((low_wind, 1), (high_wind, 10)):
                    winds = side[...].astype(F32)
                    put(at_row, level, coefs(winds[level : level + 1], winds[2 + level : 3 + level]), 0)
        row_out[0] = jnp.zeros((TILE_M, LANES), F32)
        row_out[BLOCKS + 1] = jnp.zeros((TILE_M, LANES), F32)

    if inner:
        picked, at_first, choice = ROWS, 0, row_choice(ROWS, lambda r: r)
    else:
        picked, at_first, choice = 8, 2, row_choice(8, lambda r: jnp.where(r < 4, r, r + 8))
        for level in range(2):
            for i in range(2):
                raw[level, i] = lows[level * 2 + i][...].astype(F32)
                raw[level, 10 + i] = highs[level * 2 + i][...].astype(F32)

    def reorder(group, carry):
        start = pl.multiple_of(group * 16, 16)
        for level in range(2):
            chosen = choose_rows(choice, field, start, level)
            for r in range(picked):
                raw[level, at_first + r, pl.ds(start, 16), :] = chosen[r * 16 : (r + 1) * 16]
        return carry

    lax.fori_loop(0, TILE_M // 16, reorder, 0)

    def stencil(src, level, row):
        tiles = range(TILE_M // 8)

        def block(at_row, m, j):
            return src[level, at_row, m * 8 : (m + 1) * 8, j * LANES : (j + 1) * LANES]

        here = [block(row, m, 0) for m in tiles]
        before = [None for m in tiles]
        turned_back = [pltpu.roll(here[m], LANES - 1, 1) for m in tiles]
        for j in range(BLOCKS):
            lanes = slice(j * LANES, (j + 1) * LANES)
            centre, up, down, west, east = (coef[row, level * 5 + k, :, lanes] for k in range(5))
            for m in tiles:
                turned = pltpu.roll(here[m], 1, 1)
                left = turned if j == 0 else jnp.where(first, before[m], turned)
                right = turned_back[m]
                after, after_back = None, None
                if j + 1 < BLOCKS:
                    after = block(row, m, j + 1)
                    after_back = pltpu.roll(after, LANES - 1, 1)
                    right = jnp.where(last, after_back, right)
                value = (
                    centre * here[m]
                    + up * block(row - 1, m, j)
                    + down * block(row + 1, m, j)
                    + west * left
                    + east * right
                )
                yield j, slice(m * 8, (m + 1) * 8), value
                before[m], here[m], turned_back[m] = turned, after, after_back

    def step_one(row, carry):
        for level in range(2):
            for j, members, value in stencil(raw, level, row):
                once[level, row, members, j * LANES : (j + 1) * LANES] = value
        return carry

    def step_two(row, base, slot):
        for j, members, value in stencil(once, 0, row):
            row_out[1 + j, members] = LOW_SHARE * value
        for j, members, value in stencil(once, 1, row):
            row_out[1 + j, members] = row_out[1 + j, members] + HIGH_SHARE * value
        for s in range(GROUPS):
            d = me ^ s
            for j in range(2):
                outs[s][base + j] = row_out[1 + 2 * d + j].astype(BF)
            outer = jnp.where(
                lane < HALO_R,
                row_out[2 * d + 3],
                jnp.where(lane >= LANES - HALO_R, row_out[2 * d], 0.0),
            )
            edge[s] = edge[s] + pltpu.roll(outer, HALO_R + 2 * HALO_R * slot, 1)

    def clear():
        for s in range(GROUPS):
            edge[s] = jnp.zeros((TILE_M, LANES), F32)

    def flush(at):
        for s in range(GROUPS):
            outs[s][at] = edge[s].astype(BF)

    if inner:
        lax.fori_loop(1, ROWS - 1, step_one, 0)
        for half in range(2):
            clear()

            def step(t, carry, half=half):
                step_two(2 + half * 6 + t, half * INNER + 2 * t, t)
                return carry

            lax.fori_loop(0, 6, step, 0)
            flush(half * INNER + 12)
    else:
        lax.fori_loop(1, 5, step_one, 0)
        lax.fori_loop(7, 11, step_one, 0)
        clear()

        def step(t, carry):
            under = t // 2
            step_two(2 + t + 4 * under, 2 * t + under, t)
            return carry

        lax.fori_loop(0, 4, step, 0)
        flush(4)


def observe(inner, scalars, winds, *arrays):
    steps = MINE // TILE_M
    wind_spec = pl.BlockSpec((2, 2, ROWS, WIDTH), lambda i, sc: (0, 0, 0, 0))
    specs = [pl.BlockSpec((TILE_M, 2, ROWS, WIDTH), lambda i, sc: (i, 0, 0, 0))]
    if inner:
        rows, blocks, work = ROWS, 2 * INNER, 7
        operands = arrays
    else:
        rows, blocks, work = 12, 9, 3
        side = [
            pl.BlockSpec((TILE_M, WIDTH), functools.partial(lambda k, i, sc: (k * steps + i, 0), k))
            for k in range(4)
        ] + [pl.BlockSpec((16, WIDTH), lambda i, sc: (4 * MINE // 16, 0))]
        specs = specs + side * 2
        field, low, high = arrays
        operands = [field] + [low] * 5 + [high] * 5
    return pl.pallas_call(
        functools.partial(observe_kernel, inner),
        grid_spec=pltpu.PrefetchScalarGridSpec(
            num_scalar_prefetch=1,
            grid=(steps,),
            in_specs=[wind_spec] + specs,
            out_specs=[pl.BlockSpec((blocks, TILE_M, LANES), lambda i, sc: (0, i, 0))] * GROUPS,
            scratch_shapes=[
                pltpu.VMEM((2, rows, TILE_M, WIDTH), F32),
                pltpu.VMEM((2, rows, TILE_M, WIDTH), F32),
                pltpu.VMEM((rows, 10, 8, WIDTH), F32),
                pltpu.VMEM((BLOCKS + 2, TILE_M, LANES), F32),
                pltpu.VMEM((GROUPS, TILE_M, LANES), F32),
            ],
        ),
        out_shape=[jax.ShapeDtypeStruct((blocks, MINE, LANES), BF)] * GROUPS,
        compiler_params=pltpu.CompilerParams(vmem_limit_bytes=VMEM),
        cost_estimate=pl.CostEstimate(
            flops=10**7, bytes_accessed=work * 10 * 2**20, transcendentals=0
        ),
        name="observe_inner" if inner else "observe_outer",
    )(scalars, winds, *operands)


def weights_kernel(sc, index, precision, values, spread, pull):
    me, grid_at = sc[0], sc[1]
    patch = me * OWN_PATCHES + pl.program_id(0)
    row_low = grid_at * ROWS - HALO_R
    chunk = 512
    total = jnp.zeros((6 * 32, LANES), F32)
    for c in range(K // chunk):
        at = slice(c * chunk, (c + 1) * chunk)
        cell = index[0, :, at]
        row = lax.shift_right_logical(cell, 10) - row_low
        spot = cell & (LANES - 1)
        weight = precision[0, :, at]
        parts = []
        for item in (weight, weight * values[0, :, at]):
            for _ in range(3):
                top = item.astype(BF).astype(F32)
                parts.append(top)
                item = item - top
        in_row = lax.broadcasted_iota(jnp.int32, (32, chunk), 0) == row
        at_spot = lax.broadcasted_iota(jnp.int32, (LANES, chunk), 0) == spot
        left = jnp.concatenate([jnp.where(in_row, part, 0.0) for part in parts], axis=0).astype(BF)
        right = jnp.where(at_spot, 1.0, 0.0).astype(BF)
        total = total + lax.dot_general(
            left, right, (((1,), (1,)), ((), ())), preferred_element_type=F32
        )
    weight_sum = total[0:32] + total[32:64] + total[64:96]
    value_sum = total[96:128] + total[128:160] + total[160:192]
    r = lax.broadcasted_iota(jnp.int32, (32, LANES), 0).astype(F32)
    offset = (lane_iota(32) - patch * PATCH_C + HALO_R) & (LANES - 1)
    row_diff = r - (HALO_R + (ROWS - 1) * 0.5)
    col_diff = offset.astype(F32) - (HALO_R + (PATCH_C - 1) * 0.5)
    distance = row_diff * row_diff + col_diff * col_diff
    share = jnp.exp(-distance / LOC_AREA) / (MEMBERS - 1.0)
    weight_all = weight_sum * share
    root = jnp.sqrt(weight_all)
    seen = weight_all > 0.0
    spread[0] = root
    pull[0] = jnp.where(seen, value_sum * share / jnp.where(seen, root, 1.0), 0.0)


def weigh(scalars, index, precision, values):
    spec = pl.BlockSpec((1, 1, K), lambda p, sc: (p, 0, 0))
    out = pl.BlockSpec((1, 32, LANES), lambda p, sc: (p, 0, 0))
    shape = jax.ShapeDtypeStruct((OWN_PATCHES, 32, LANES), F32)
    spread, pull = pl.pallas_call(
        weights_kernel,
        grid_spec=pltpu.PrefetchScalarGridSpec(
            num_scalar_prefetch=1,
            grid=(OWN_PATCHES,),
            in_specs=[spec] * 3,
            out_specs=[out] * 2,
        ),
        out_shape=[shape] * 2,
        compiler_params=pltpu.CompilerParams(vmem_limit_bytes=VMEM),
        cost_estimate=pl.CostEstimate(flops=10**9, bytes_accessed=2**18, transcendentals=0),
        name="weigh",
    )(
        scalars,
        index.reshape(OWN_PATCHES, 1, K),
        precision.reshape(OWN_PATCHES, 1, K),
        values.reshape(OWN_PATCHES, 1, K),
    )
    return spread, pull


def own_plan():
    return [
        [(half * INNER + 2 * t, half * INNER + 12, t, 10 + 6 * half + t) for t in range(6)]
        for half in range(2)
    ]


def inner_plan():
    low = [(2 * t, 12, t, t) for t in range(6)]
    high = [(INNER + 2 * t, INNER + 12, t, 26 + t) for t in range(6)]
    at = 2 * INNER
    outer = [(at + 2 * t, at + 4, t, 8 + t) for t in range(2)]
    outer += [(at + 5 + 2 * t, at + 4, 2 + t, 22 + t) for t in range(2)]
    return [low, high, outer]


def outer_plan():
    rows = [(1 + 2 * t, 0, 2 + t, 6 + t) for t in range(2)]
    rows += [(OUTER + 2 * t, OUTER + 4, t, 24 + t) for t in range(2)]
    return [rows]


def gram_rows(plan, patches, spread, pull, cells, scaled, mean_of, total):
    lane_row = lane_iota(1)
    lane = lane_iota(MINE)
    at_top = lax.broadcasted_iota(jnp.int32, (16, LANES), 0) == 0

    def pick(p, first, second, outer, lanes):
        low_edge = lanes < HALO_R
        high_edge = lanes >= LANES - HALO_R
        if p == 0:
            return jnp.where(high_edge, outer, first)
        if p == 1:
            return jnp.where(low_edge, second, first)
        if p == 2:
            return jnp.where(high_edge, first, second)
        return jnp.where(low_edge, outer, second)

    ones = jnp.full((8, MEMBERS), 1.0, BF)
    used = set()
    for chunk in plan:
        for at, edge_at, _, _ in chunk:
            used |= {at, at + 1, edge_at}
    for at in sorted(used):
        summed = jnp.dot(
            ones, cells[at].reshape(MEMBERS, LANES), preferred_element_type=F32
        )
        mean_of[at] = summed / MEMBERS

    def multiply(c, i, width):
        total[i] = total[i] + lax.dot_general(
            scaled[c, i, :, 0:width],
            scaled[c, i, 0:MEMBERS, 0:width],
            (((1,), (1,)), ((), ())),
            preferred_element_type=F32,
        )

    waiting = []
    for c, chunk in enumerate(plan):
        for n, (at, edge_at, slot, window_row) in enumerate(chunk):
            back = LANES - HALO_R - 2 * HALO_R * slot
            outer_mean = pltpu.roll(mean_of[edge_at], back, 1)[0:1]
            first_mean, second_mean = mean_of[at, 0:1, :], mean_of[at + 1, 0:1, :]
            place = slice(n * LANES, (n + 1) * LANES)
            means, roots = [], []
            for i, p in enumerate(patches):
                mean = pick(p, first_mean, second_mean, outer_mean, lane_row)
                root = spread[p, window_row : window_row + 1, :]
                innov = pull[p, window_row : window_row + 1, :] - root * mean
                scaled[c, i, MEMBERS : MEMBERS + 16, place] = jnp.where(at_top, innov, 0.0).astype(BF)
                means.append(mean)
                roots.append(root)
            for group in range(GROUPS):
                first = cells[at, group].astype(F32)
                second = cells[at + 1, group].astype(F32)
                outer = pltpu.roll(cells[edge_at, group].astype(F32), back, 1)
                for i, p in enumerate(patches):
                    picked = pick(p, first, second, outer, lane)
                    scaled[c, i, group * MINE : (group + 1) * MINE, place] = (
                        (picked - means[i]) * roots[i]
                    ).astype(BF)
            if waiting:
                multiply(*waiting.pop(0))
        for ready in waiting:
            multiply(*ready)
        waiting = [(c, i, len(chunk) * LANES) for i in range(len(patches))]
    for ready in waiting:
        multiply(*ready)


def fetch_all(moves, cells, sems, meanwhile):
    copies = []
    for n, (src, at, count, group) in enumerate(moves):
        copy = pltpu.make_async_copy(src, cells.at[pl.ds(at, count), group], sems.at[n])
        copy.start()
        copies.append(copy)
    meanwhile()
    for copy in copies:
        copy.wait()


def own_kernel(sc, spread, pull, *refs):
    pieces, totals = refs[0:4], refs[4:6]
    cells, scaled, mean_of, total, sems = refs[6:]
    me = sc[0]

    def clear():
        total[...] = jnp.zeros_like(total)

    fetch_all([(pieces[s], 0, 2 * INNER, me ^ s) for s in range(GROUPS)], cells, sems, clear)
    gram_rows(own_plan(), list(range(OWN_PATCHES)), spread, pull, cells, scaled, mean_of, total)
    for i in range(OWN_PATCHES):
        totals[i // PAIR][i % PAIR] = total[i]


def inner_kernel(sc, spread, pull, *refs):
    before, near, far, outer, totals = refs[0:2], refs[2:4], refs[4:6], refs[6:10], refs[10:12]
    cells, scaled, mean_of, total, sems = refs[12:]
    me = sc[0]
    moves = []
    for side in range(2):
        for s in range(GROUPS):
            moves.append(((near, far)[s // 2][side].at[s % 2], side * INNER, INNER, me ^ s))
    for s in range(GROUPS):
        moves.append((outer[s], 2 * INNER, 9, me ^ s))

    def begin():
        for i in range(OWN_PATCHES):
            total[i] = before[i // PAIR][i % PAIR]

    fetch_all(moves, cells, sems, begin)
    gram_rows(inner_plan(), list(range(OWN_PATCHES)), spread, pull, cells, scaled, mean_of, total)
    for i in range(OWN_PATCHES):
        totals[i // PAIR][i % PAIR] = total[i]


def running_gram(kernel, plan, name, scalars, spread, pull, before, pieces):
    vmem = pl.BlockSpec(memory_space=pltpu.VMEM)
    anywhere = pl.BlockSpec(memory_space=pl.ANY)
    blocks = 2 * INNER + 9 * (len(plan) - 2)
    return pl.pallas_call(
        kernel,
        in_specs=[pl.BlockSpec(memory_space=pltpu.SMEM)]
        + [vmem] * (2 + len(before))
        + [anywhere] * len(pieces),
        out_specs=[vmem] * 2,
        out_shape=[jax.ShapeDtypeStruct((PAIR, MEMBERS + 16, MEMBERS), F32)] * 2,
        scratch_shapes=[
            pltpu.VMEM((blocks, GROUPS, MINE, LANES), BF),
            pltpu.VMEM((len(plan), OWN_PATCHES, MEMBERS + 16, 6 * LANES), BF),
            pltpu.VMEM((blocks, 8, LANES), F32),
            pltpu.VMEM((OWN_PATCHES, MEMBERS + 16, MEMBERS), F32),
            pltpu.SemaphoreType.DMA((12,)),
        ],
        compiler_params=pltpu.CompilerParams(vmem_limit_bytes=VMEM),
        cost_estimate=pl.CostEstimate(flops=10**7, bytes_accessed=35 * 2**20, transcendentals=0),
        name=name,
    )(scalars, spread, pull, *before, *pieces)


def last_kernel(patches, sc, spread, pull, before, low, high, *refs):
    outs = refs[0:4]
    cells, scaled, mean_of, total, sems = refs[4:]
    me = sc[0]
    moves = []
    for s in range(GROUPS):
        moves.append((low.at[s], 0, OUTER, me ^ s))
        moves.append((high.at[s], OUTER, OUTER, me ^ s))

    def begin():
        total[...] = before[...]

    fetch_all(moves, cells, sems, begin)
    gram_rows(outer_plan(), patches, spread, pull, cells, scaled, mean_of, total)
    for s in range(GROUPS):
        at = pl.multiple_of((me ^ s) * MINE, MINE)
        extra = []
        for i in range(PAIR):
            projected = total[i, MEMBERS : MEMBERS + 8, pl.ds(at, MINE)]
            top = projected.astype(BF).astype(F32)
            extra += [top, projected - top]
            block = total[i, pl.ds(at, MINE), :]
            outs[s][i * MINE : (i + 1) * MINE, :] = block.astype(outs[s].dtype)
        extra = jnp.concatenate(extra, axis=1)
        if s > 0:
            extra = jnp.concatenate([extra, extra], axis=0).astype(BF)
        outs[s][PAIR * MINE :, :] = extra


def last_gram(patches, scalars, spread, pull, before, low, high):
    vmem = pl.BlockSpec(memory_space=pltpu.VMEM)
    anywhere = pl.BlockSpec(memory_space=pl.ANY)
    rows = PAIR * MINE
    return pl.pallas_call(
        functools.partial(last_kernel, patches),
        in_specs=[pl.BlockSpec(memory_space=pltpu.SMEM), vmem, vmem, vmem] + [anywhere] * 2,
        out_specs=[vmem] * GROUPS,
        out_shape=[jax.ShapeDtypeStruct((rows + 8, MEMBERS), F32)]
        + [jax.ShapeDtypeStruct((rows + 16, MEMBERS), BF)] * (GROUPS - 1),
        scratch_shapes=[
            pltpu.VMEM((2 * OUTER, GROUPS, MINE, LANES), BF),
            pltpu.VMEM((1, PAIR, MEMBERS + 16, 4 * LANES), BF),
            pltpu.VMEM((2 * OUTER, 8, LANES), F32),
            pltpu.VMEM((PAIR, MEMBERS + 16, MEMBERS), F32),
            pltpu.SemaphoreType.DMA((8,)),
        ],
        compiler_params=pltpu.CompilerParams(vmem_limit_bytes=VMEM),
        cost_estimate=pl.CostEstimate(flops=10**7, bytes_accessed=20 * 2**20, transcendentals=0),
        name=f"gram_last_{patches[0]}",
    )(scalars, spread, pull, before, low, high)


def assemble_kernel(which, sc, *refs):
    gram, proj = refs[-2], refs[-1]
    for n, s in enumerate(which):

        @pl.when(pl.program_id(0) == n)
        def _(n=n, s=s):
            for p in range(PAIR):
                gram[p] = refs[n][p * MINE : (p + 1) * MINE, :].astype(F32)
                at = p * 2 * MINE
                extra = refs[n][PAIR * MINE :, at : at + 2 * MINE].astype(F32)
                proj[0, p : p + 1, :] = extra[0:1, 0:MINE] + extra[0:1, MINE:]


def assemble(half, which, scalars, parts, begun):
    def at(n, sc):
        return ((sc[0] ^ (n + which[0])) * 2 + half, 0, 0)

    begun = [] if begun is None else list(begun)
    count = len(which)
    return pl.pallas_call(
        functools.partial(assemble_kernel, which),
        grid_spec=pltpu.PrefetchScalarGridSpec(
            num_scalar_prefetch=1,
            grid=(count,),
            in_specs=[pl.BlockSpec(parts[s].shape, lambda n, sc: (0, 0)) for s in which]
            + [pl.BlockSpec(memory_space=pl.ANY)] * len(begun),
            out_specs=[
                pl.BlockSpec((PAIR, MINE, MEMBERS), at),
                pl.BlockSpec((1, PAIR, MINE), at),
            ],
        ),
        out_shape=[
            jax.ShapeDtypeStruct((GROUPS * OWN_PATCHES, MINE, MEMBERS), F32),
            jax.ShapeDtypeStruct((2 * GROUPS, PAIR, MINE), F32),
        ],
        input_output_aliases={count + 1: 0, count + 2: 1} if begun else {},
        compiler_params=pltpu.CompilerParams(vmem_limit_bytes=VMEM),
        cost_estimate=pl.CostEstimate(flops=10**6, bytes_accessed=count * 2**20, transcendentals=0),
        name=f"assemble_{half}_{which[0]}",
    )(scalars, *[parts[s] for s in which], *begun)


def bundle_kernel(plan, count, arrays, *refs):
    sources, outs, sems = refs[:arrays], refs[arrays : arrays + 2], refs[arrays + 2]
    copies = []
    for out, starts in zip(outs, plan):
        for k, start in enumerate(starts):
            source = sources[k].at[pl.ds(start, count)]
            copies.append(pltpu.make_async_copy(source, out.at[k], sems.at[len(copies)]))
    for copy in copies:
        copy.start()
    for copy in copies:
        copy.wait()


def bundle(name, pieces, count, low_start, high_start):
    n = len(pieces)
    plan = ([low_start] * n, [high_start] * n)
    anywhere = pl.BlockSpec(memory_space=pl.ANY)
    return pl.pallas_call(
        functools.partial(bundle_kernel, plan, count, n),
        in_specs=[anywhere] * n,
        out_specs=[pl.BlockSpec(memory_space=pltpu.VMEM)] * 2,
        out_shape=[jax.ShapeDtypeStruct((n, count, MINE, LANES), BF)] * 2,
        scratch_shapes=[pltpu.SemaphoreType.DMA((2 * n,))],
        compiler_params=pltpu.CompilerParams(vmem_limit_bytes=VMEM),
        cost_estimate=pl.CostEstimate(flops=0, bytes_accessed=4 * 2**20, transcendentals=0),
        name=name,
    )(*pieces)


def after(*arrays):
    return lax.optimization_barrier(arrays)


def per_device(field, winds, obs_index, measured_values, precision_weights):
    grid_size = lax.axis_size("grid")
    me = lax.axis_index("mem")
    scalars = jnp.stack([me, lax.axis_index("grid")]).astype(jnp.int32)
    forward = [(i, i + 1) for i in range(grid_size - 1)]
    backward = [(i + 1, i) for i in range(grid_size - 1)]

    def swap(x, s):
        return lax.ppermute(x, "mem", [(i, i ^ s) for i in range(GROUPS)])

    def exchange(pieces):
        far = [swap(pieces[s], s) for s in (2, 3)]
        return [pieces[0], swap(pieces[1], 1)] + far

    top, bottom = edges(winds, field)
    low = lax.ppermute(bottom, "grid", forward)
    high = lax.ppermute(top, "grid", backward)

    inner = observe(True, scalars, winds, field)
    low, high, *inner = after(low, high, *inner)
    far_inner = [swap(inner[s], s) for s in (2, 3)]
    near_inner = [inner[0], swap(inner[1], 1)]
    near_up, near_down = bundle("bundle_near", near_inner, INNER, INNER, 0)
    near_up, near_down, low, obs_index, measured_values, precision_weights = after(
        near_up, near_down, low, obs_index, measured_values, precision_weights
    )
    near_low = lax.ppermute(near_up, "grid", forward)
    near_high = lax.ppermute(near_down, "grid", backward)

    outer = observe(False, scalars, winds, field, low, high)

    def mine(x):
        return lax.dynamic_slice_in_dim(x, me * OWN_PATCHES, OWN_PATCHES, 0)

    spread, pull = weigh(scalars, mine(obs_index), mine(precision_weights), mine(measured_values))

    far_inner[0], far_inner[1], spread, pull, *outer = after(*far_inner, spread, pull, *outer)
    far_up, far_down = bundle("bundle_far", far_inner, INNER, INNER, 0)
    totals = running_gram(
        own_kernel, own_plan(), "gram_own", scalars, spread, pull, [], near_inner + far_inner
    )
    near_low, near_high, far_up, far_down, *rest = after(
        near_low, near_high, far_up, far_down, *totals, *outer
    )
    totals, outer = rest[:2], rest[2:]
    far_outer = [swap(outer[s], s) for s in (2, 3)]
    far_up, far_down, core_outer = after(far_up, far_down, swap(outer[1], 1))
    outer = [outer[0], core_outer] + far_outer
    far_low = lax.ppermute(far_up, "grid", forward)
    far_high = lax.ppermute(far_down, "grid", backward)
    outer_up, outer_down = bundle("bundle_outer", outer, OUTER, 4, 0)
    outer_low = lax.ppermute(outer_up, "grid", forward)
    outer_high = lax.ppermute(outer_down, "grid", backward)

    halos = [near_low, near_high, far_low, far_high, *outer]
    totals = running_gram(
        inner_kernel, inner_plan(), "gram_inner", scalars, spread, pull, totals, halos
    )
    result = None
    for n in range(2):
        patches = [PAIR * n, PAIR * n + 1]
        sent = last_gram(
            patches, scalars, spread, pull, totals[n], outer_low, outer_high
        )
        parts = exchange(sent)
        for which in ([0, 1, 2, 3],) if n == 0 else ([0, 1], [2], [3]):
            result = assemble(n, which, scalars, parts, result)
    return result[0], result[1].reshape(GROUPS * OWN_PATCHES, MINE)


def solution(mesh):
    return jax.shard_map(
        per_device,
        mesh=mesh,
        in_specs=(
            P("mem", None, "grid", None),
            P(None, None, "grid", None),
            P("grid", None),
            P("grid", None),
            P("grid", None),
        ),
        out_specs=(P("grid", "mem", None), P("grid", "mem")),
        check_vma=False,
    )
```
